32 devices in a mesh: row: 8 (over y, x, core), col: 4 (over z).
Axes of the slice: x: 2, y: 2, z: 4, core: 2. Of those that a mesh axis runs over, the one named last changes fastest.
Arguments:
- queries: bfloat16 [4096, 512], P(('row', 'col')), may hold values from -6 to 6
- grad_out: bfloat16 [4096, 512], P(('row', 'col')), may hold values from -6 to 6
- attn_out: bfloat16 [4096, 512], P(('row', 'col')), may hold values from -2 to 2
- key_states: bfloat16 [4096, 128], P(('row', 'col')), may hold values from -6 to 6
- value_states: bfloat16 [4096, 128], P(('row', 'col')), may hold values from -2 to 2
- log_norm: float32 [4096, 4], P(('row', 'col')), as said below
- position: int32 [4096], replicated, may hold values from 0 to 2047, as said below
- modality: int32 [4096], replicated, may hold values from 0 to 2, as said below
- bidirectional: int32 [3, 3], replicated, may hold values from 0 to 1
Outputs:
- grad_query: bfloat16 [4096, 512], P(('row', 'col'))
- grad_key: bfloat16 [4096, 128], P(('row', 'col'))
- grad_value: bfloat16 [4096, 128], P(('row', 'col'))
The draws below stay inside these ranges and needn't reach their ends.
Inputs may be any that keep to these rules, and one draw needn't show every extreme that they name: `position`: within each sequence a permutation of 0 to 2047, token t belonging to sequence (t // 128) % 4 // 2; the tokens of one device hold two runs of 64 consecutive positions. `modality`: the same for all tokens of one sequence within one span of 32 consecutive positions. `log_norm`: the log of the number of keys that the token may see, plus 0.25 to 0.75.
All inputs are finite; a program needn't handle non-finite values.
Results may differ from the reference program's by a relative error of at most 0.0052.
Values may be sent and summed in bfloat16 or wider, within the bound.
A program may use at most 64 MiB of HBM per device.

```python
import functools
import math
import jax
import jax.numpy as jnp
from jax import lax

HEADS = 4
HEAD_DIM = 128
TOK_DEV = 128
SEQS = 2
SEQ_LEN = 2048
TOKENS = 4096
UNIT = 64
SPAN = 32
N_ROW = 8


def shared_layout(key):
    base = jax.random.fold_in(key, 4242)
    key_order, key_mod, key_table = jax.random.split(base, 3)
    block_count = SEQ_LEN // TOK_DEV

    def one_order(order_key):
        return jax.random.permutation(order_key, block_count)
    order = jax.vmap(one_order)(jax.random.split(key_order, SEQS)).astype(jnp.int32)
    token = jnp.arange(TOKENS, dtype=jnp.int32)
    block = token // TOK_DEV
    seq_tok = block % (2 * SEQS) // 2
    local_block = block // (2 * SEQS) * 2 + block % 2
    offset = token % TOK_DEV
    first = order[seq_tok, local_block]
    position = jnp.where(offset < UNIT, first * UNIT + offset, (2 * block_count - 1 - first) * UNIT + offset - UNIT)
    span_mod = jax.random.randint(key_mod, (SEQS, SEQ_LEN // SPAN + 1), 0, 3, dtype=jnp.int32)
    pos_mod = span_mod[:, jnp.arange(SEQ_LEN, dtype=jnp.int32) // SPAN]
    modality = pos_mod[seq_tok, position]
    table = jax.random.randint(key_table, (3, 3), 0, 2, dtype=jnp.int32)
    table = table.at[0, 0].set(0).at[1, 1].set(1)
    return (position.astype(jnp.int32), modality.astype(jnp.int32), table, pos_mod, seq_tok)


def draw_position(key, part):
    return shared_layout(key)[0]


def draw_modality(key, part):
    return shared_layout(key)[1]


def draw_bidirectional(key, part):
    return shared_layout(key)[2]


def draw_log_norm(key, part):
    position, modality, table, pos_mod, seq_tok = shared_layout(key)
    unit_mod = pos_mod.reshape(SEQS, SEQ_LEN // UNIT, UNIT)
    slots = jnp.arange(UNIT, dtype=jnp.int32)
    later = slots[None, :] > slots[:, None]
    pair = table[unit_mod[:, :, :, None], unit_mod[:, :, None, :]] == 1
    extra = jnp.sum(jnp.where(later[None, None, :, :] & pair, 1, 0), axis=3).reshape(SEQS, SEQ_LEN)
    count_pos = jnp.arange(SEQ_LEN, dtype=jnp.int32)[None, :] + 1 + extra
    count_tok = count_pos[seq_tok, position]
    noise = jax.random.uniform(jax.random.fold_in(key, 99), (TOKENS, HEADS), jnp.float32, -0.25, 0.25)
    return jnp.log(count_tok.astype(jnp.float32))[:, None] + 0.5 + noise


def block_scale(rng, extent, cuts, least, largest):
    gain, own = 1.0, jax.random.fold_in(rng, 6)
    for axis_at, blocks in cuts:
        draws = jnp.exp(jax.random.uniform(jax.random.fold_in(own, axis_at), (blocks,), jnp.float32, least / len(cuts), largest / len(cuts)))
        gain = gain * jnp.repeat(draws, extent[axis_at] // blocks).reshape([-1 if axis == axis_at else 1 for axis in range(len(extent))])
    return gain


def gaussian(own_key, extent, spread, limit, cuts=(), held_as=jnp.bfloat16):
    entries = spread * jax.random.normal(own_key, extent, jnp.float32)
    if cuts:
        entries = entries * block_scale(own_key, extent, cuts, -0.22, 0.18)
    return jnp.clip(entries, -limit, limit).astype(held_as)


def setup_inputs(seed: int = 0) -> dict:
    arg_keys = jax.random.split(jax.random.key(seed), 10)
    queries = gaussian(arg_keys[0], (TOKENS, HEADS * HEAD_DIM), 1.0, 6.0, ((0, 32),))
    grad_out = gaussian(arg_keys[1], (TOKENS, HEADS * HEAD_DIM), 1.0, 6.0, ((0, 32),))
    attn_out = gaussian(arg_keys[2], (TOKENS, HEADS * HEAD_DIM), 0.3, 2.0, ((0, 32),))
    key_states = gaussian(arg_keys[3], (TOKENS, HEAD_DIM), 1.0, 6.0, ((0, 32),))
    value_states = gaussian(arg_keys[4], (TOKENS, HEAD_DIM), 0.3, 2.0, ((0, 32),))
    log_norm = draw_log_norm(jax.random.fold_in(arg_keys[9], 71), 0)
    position = draw_position(jax.random.fold_in(arg_keys[9], 71), 0)
    modality = draw_modality(jax.random.fold_in(arg_keys[9], 71), 0)
    bidirectional = draw_bidirectional(jax.random.fold_in(arg_keys[9], 71), 0)
    return dict(queries=queries, grad_out=grad_out, attn_out=attn_out, key_states=key_states, value_states=value_states, log_norm=log_norm, position=position, modality=modality, bidirectional=bidirectional)


def split_seqs(array):
    tail = array.shape[1:]
    grid = array.reshape((N_ROW, SEQS, 2 * TOK_DEV) + tail)
    return jnp.moveaxis(grid, 1, 0).reshape((SEQS, SEQ_LEN) + tail)


def join_seqs(array):
    tail = array.shape[2:]
    grid = array.reshape((SEQS, N_ROW, 2 * TOK_DEV) + tail)
    return jnp.moveaxis(grid, 0, 1).reshape((TOKENS,) + tail)


def tile_grads(q_rows, d_rows, lse_rows, delta_rows, q_pos, q_mod, key_states, value_states, position, modality, table):
    row_count = q_rows.shape[0]
    flat_q = q_rows.reshape(row_count * HEADS, HEAD_DIM)
    flat_d = d_rows.reshape(row_count * HEADS, HEAD_DIM)
    score_scale = HEAD_DIM ** -0.5
    scores = jnp.dot(flat_q, key_states.T, preferred_element_type=jnp.float32) * score_scale
    causal = position[None, :] <= q_pos[:, None]
    same_unit = (position[None, :] // UNIT) == (q_pos[:, None] // UNIT)
    pair_bid = table[q_mod[:, None], modality[None, :]] == 1
    allowed = jnp.repeat(causal | (same_unit & pair_bid), HEADS, axis=0)
    attn_probs = jnp.where(allowed, jnp.exp(scores - lse_rows.reshape(-1, 1)), 0.0)
    probs_low = attn_probs.astype(jnp.bfloat16)
    grad_probs = jnp.dot(flat_d, value_states.T, preferred_element_type=jnp.float32)
    grad_scores = attn_probs * (grad_probs - delta_rows.reshape(-1, 1))
    scores_low = grad_scores.astype(jnp.bfloat16)
    grad_q = jnp.dot(scores_low, key_states, preferred_element_type=jnp.float32) * score_scale
    grad_k = jnp.dot(scores_low.T, flat_q, preferred_element_type=jnp.float32) * score_scale
    grad_v = jnp.dot(probs_low.T, flat_d, preferred_element_type=jnp.float32)
    return grad_q.reshape(row_count, HEADS * HEAD_DIM), grad_k, grad_v


def sequence_grads(table, pieces):
    queries, grad_out, row_delta, key_states, value_states, log_norm, position, modality = pieces
    block_len = math.gcd(SEQ_LEN, 512)

    def step_fn(totals, block_index):
        start = (block_index * block_len).astype(jnp.int32)
        q_rows = lax.dynamic_slice_in_dim(queries, start, block_len)
        d_rows = lax.dynamic_slice_in_dim(grad_out, start, block_len)
        lse_rows = lax.dynamic_slice_in_dim(log_norm, start, block_len)
        delta_rows = lax.dynamic_slice_in_dim(row_delta, start, block_len)
        q_pos = lax.dynamic_slice_in_dim(position, start, block_len)
        q_mod = lax.dynamic_slice_in_dim(modality, start, block_len)
        grad_q, grad_k, grad_v = tile_grads(q_rows, d_rows, lse_rows, delta_rows, q_pos, q_mod,
                                            key_states, value_states, position, modality, table)
        return (totals[0] + grad_k, totals[1] + grad_v), grad_q

    empty = jnp.zeros((SEQ_LEN, HEAD_DIM), jnp.float32)
    totals, grad_blocks = lax.scan(step_fn, (empty, empty), jnp.arange(SEQ_LEN // block_len, dtype=jnp.int32))
    return grad_blocks.reshape(SEQ_LEN, HEADS * HEAD_DIM), totals[0], totals[1]


def reference(queries, grad_out, attn_out, key_states, value_states, log_norm, position, modality, bidirectional):
    row_delta = jnp.einsum(
        "thd,thd->th",
        grad_out.astype(jnp.float32).reshape(TOKENS, HEADS, HEAD_DIM),
        attn_out.astype(jnp.float32).reshape(TOKENS, HEADS, HEAD_DIM),
    )
    pieces = tuple(split_seqs(array) for array in
                   (queries, grad_out, row_delta, key_states, value_states, log_norm, position, modality))
    grad_q, grad_k, grad_v = lax.map(functools.partial(sequence_grads, bidirectional), pieces)
    return (join_seqs(grad_q).astype(jnp.bfloat16), join_seqs(grad_k).astype(jnp.bfloat16),
            join_seqs(grad_v).astype(jnp.bfloat16))
```

```python
import functools

import jax
import jax.numpy as jnp
from jax import lax
from jax.experimental import pallas as pl
from jax.experimental.pallas import tpu as pltpu
from jax.sharding import PartitionSpec as P

UNIT = 64
LOG2E = 1.4426950408889634
MASKED = -1e30
MESH = pl.DeviceIdType.MESH


def contract_first(left, right):
    return lax.dot_general(
        left, right, (((0,), (0,)), ((), ())), preferred_element_type=jnp.float32
    )


def contract_last(left, right):
    return lax.dot_general(
        left, right, (((1,), (1,)), ((), ())), preferred_element_type=jnp.float32
    )


def kernel(
    row_size,
    col_size,
    heads,
    q_ref,
    d_ref,
    o_ref,
    k_ref,
    v_ref,
    lse_ref,
    pos_ref,
    mod_ref,
    table_ref,
    gq_ref,
    gk_ref,
    gv_ref,
    qd,
    aux,
    kv,
    acc,
    out_kv,
    in_kv,
    acc_q,
    out_q,
    in_q,
    kv_send,
    kv_recv,
    qd_send,
    qd_recv,
    grad_send,
    grad_recv,
    q_send,
    q_recv,
):
    me = lax.axis_index("row")
    col = lax.axis_index("col")
    mate = col + 1 - 2 * (col % 2)
    tokens, width = k_ref.shape
    scale = width ** (-0.5)

    def ahead(step):
        return lax.rem(me + step, row_size)

    def behind(step):
        return lax.rem(me - step + row_size, row_size)

    barrier = pltpu.get_barrier_semaphore()

    def greet(step, carry):
        pl.semaphore_signal(barrier, inc=1, device_id={"row": ahead(step)}, device_id_type=MESH)
        return carry

    lax.fori_loop(1, row_size, greet, 0)
    pl.semaphore_signal(barrier, inc=1, device_id={"col": mate}, device_id_type=MESH)

    kv[0, 0] = k_ref[...]
    kv[0, 1] = v_ref[...]
    for h in range(heads):
        lanes = slice(h * width, (h + 1) * width)
        rows = slice(h * tokens, (h + 1) * tokens)
        qd[0, 0, rows, :] = q_ref[:, lanes]
        qd[0, 1, rows, :] = d_ref[:, lanes]
        product = d_ref[:, lanes].astype(jnp.float32) * o_ref[:, lanes].astype(jnp.float32)
        aux[0, heads + h : heads + h + 1, :] = jnp.sum(product.T, axis=0, keepdims=True)
    aux[0, 0:heads, :] = lse_ref[...] * LOG2E

    pl.semaphore_wait(barrier, row_size)

    def kv_copy(step):
        return pltpu.make_async_remote_copy(
            src_ref=kv.at[0],
            dst_ref=kv.at[step],
            send_sem=kv_send.at[step],
            recv_sem=kv_recv.at[step],
            device_id={"row": ahead(step)},
            device_id_type=MESH,
        )

    def grad_copy(step):
        return pltpu.make_async_remote_copy(
            src_ref=out_kv.at[step],
            dst_ref=in_kv.at[step],
            send_sem=grad_send.at[step],
            recv_sem=grad_recv.at[step],
            device_id={"row": behind(step)},
            device_id_type=MESH,
        )

    def to_mate(source, target, send_sem, recv_sem):
        return pltpu.make_async_remote_copy(
            src_ref=source,
            dst_ref=target,
            send_sem=send_sem,
            recv_sem=recv_sem,
            device_id={"col": mate},
            device_id_type=MESH,
        )

    pair_copies = [
        to_mate(qd.at[0], qd.at[1], qd_send.at[0], qd_recv.at[0]),
        to_mate(aux.at[0], aux.at[1], qd_send.at[1], qd_recv.at[1]),
    ]
    q_copy = to_mate(out_q, in_q, q_send, q_recv)

    def send_kv(step, carry):
        kv_copy(step).start()
        return carry

    lax.fori_loop(1, row_size, send_kv, 0)
    for copy in pair_copies:
        copy.start()

    def limits(which_col):
        at = me * col_size + which_col
        pos = pos_ref[pl.ds(at, 1), :]
        mod = mod_ref[pl.ds(at, 1), :]
        last = pos - lax.rem(pos, UNIT) + (UNIT - 1)
        out = []
        for m in range(3):
            seen = jnp.where(
                mod == 0, table_ref[0, m], jnp.where(mod == 1, table_ref[1, m], table_ref[2, m])
            )
            out.append(jnp.where(seen == 1, last, pos))
        return out

    def bias(step, limit):
        at = behind(step) * col_size + col
        shape = (tokens, tokens)
        pos = jnp.broadcast_to(pos_ref[pl.ds(at, 1), :], shape).T
        mod = jnp.broadcast_to(mod_ref[pl.ds(at, 1), :], shape).T
        bound = jnp.where(mod == 0, limit[0], jnp.where(mod == 1, limit[1], limit[2]))
        return jnp.where(pos <= bound, 0.0, MASKED)

    def tile(half, step, limit):
        flat_q = qd[half, 0]
        flat_d = qd[half, 1]
        keys = kv[step, 0]
        values = kv[step, 1]
        lse = jnp.concatenate([aux[half, h : h + 1, :] for h in range(heads)], axis=1)
        delta = jnp.concatenate(
            [aux[half, heads + h : heads + h + 1, :] for h in range(heads)], axis=1
        )
        hidden = jnp.concatenate([bias(step, limit)] * heads, axis=1)
        scores = contract_last(keys, flat_q)
        probs = jnp.exp2(scores * (scale * LOG2E) - lse + hidden)
        grad_probs = contract_last(values, flat_d)
        probs_low = probs.astype(jnp.bfloat16)
        scores_low = (probs * (grad_probs - delta)).astype(jnp.bfloat16)
        grad_v = jnp.dot(probs_low, flat_d, preferred_element_type=jnp.float32)
        grad_k = jnp.dot(scores_low, flat_q, preferred_element_type=jnp.float32)
        grad_q = contract_first(scores_low, keys)
        return grad_q, grad_k, grad_v

    acc_q[...] = jnp.zeros_like(acc_q)
    own_limit = limits(col)
    mate_limit = limits(mate)

    def own_step(step, carry):
        @pl.when(step > 0)
        def _():
            kv_copy(step).wait_recv()

        grad_q, grad_k, grad_v = tile(0, step, own_limit)
        acc_q[0] += grad_q
        acc[step, 0] = grad_k
        acc[step, 1] = grad_v
        return carry

    lax.fori_loop(0, row_size, own_step, 0)

    for copy in pair_copies:
        copy.wait_recv()

    def mate_step(i, carry):
        step = lax.rem(i + 1, row_size)
        grad_q, grad_k, grad_v = tile(1, step, mate_limit)
        acc_q[1] += grad_q
        grad_k = grad_k + acc[step, 0]
        grad_v = grad_v + acc[step, 1]

        @pl.when(step > 0)
        def _():
            out_kv[step, 0] = grad_k.astype(jnp.bfloat16)
            out_kv[step, 1] = grad_v.astype(jnp.bfloat16)
            grad_copy(step).start()

        @pl.when(step == 0)
        def _():
            acc[0, 0] = grad_k
            acc[0, 1] = grad_v

        return carry

    lax.fori_loop(0, row_size, mate_step, 0)

    out_q[...] = acc_q[1].astype(jnp.bfloat16)
    q_copy.start()

    def gather(step, carry):
        grad_copy(step).wait_recv()
        acc[0] += in_kv[step].astype(jnp.float32)
        return carry

    lax.fori_loop(1, row_size, gather, 0)
    gk_ref[...] = (acc[0, 0] * scale).astype(jnp.bfloat16)
    gv_ref[...] = acc[0, 1].astype(jnp.bfloat16)

    q_copy.wait_recv()
    for h in range(heads):
        rows = slice(h * tokens, (h + 1) * tokens)
        total = acc_q[0, rows, :] + in_q[rows, :].astype(jnp.float32)
        gq_ref[:, h * width : (h + 1) * width] = (total * scale).astype(jnp.bfloat16)

    def settle(step, carry):
        kv_copy(step).wait_send()
        grad_copy(step).wait_send()
        return carry

    lax.fori_loop(1, row_size, settle, 0)
    for copy in pair_copies:
        copy.wait_send()
    q_copy.wait_send()


def shards(
    queries,
    grad_out,
    attn_out,
    key_states,
    value_states,
    log_norm,
    position,
    modality,
    bidirectional,
):
    tokens, width = key_states.shape
    heads = log_norm.shape[1]
    row_size = lax.axis_size("row")
    col_size = lax.axis_size("col")
    flat = heads * tokens
    vmem = pl.BlockSpec(memory_space=pltpu.VMEM)
    smem = pl.BlockSpec(memory_space=pltpu.SMEM)
    pairs = row_size * tokens * flat * 2
    return pl.pallas_call(
        functools.partial(kernel, row_size, col_size, heads),
        out_shape=(
            jax.ShapeDtypeStruct(queries.shape, jnp.bfloat16),
            jax.ShapeDtypeStruct(key_states.shape, jnp.bfloat16),
            jax.ShapeDtypeStruct(value_states.shape, jnp.bfloat16),
        ),
        in_specs=[vmem] * 8 + [smem],
        out_specs=(vmem, vmem, vmem),
        scratch_shapes=[
            pltpu.VMEM((2, 2, flat, width), jnp.bfloat16),
            pltpu.VMEM((2, 2 * heads, tokens), jnp.float32),
            pltpu.VMEM((row_size, 2, tokens, width), jnp.bfloat16),
            pltpu.VMEM((row_size, 2, tokens, width), jnp.float32),
            pltpu.VMEM((row_size, 2, tokens, width), jnp.bfloat16),
            pltpu.VMEM((row_size, 2, tokens, width), jnp.bfloat16),
            pltpu.VMEM((2, flat, width), jnp.float32),
            pltpu.VMEM((flat, width), jnp.bfloat16),
            pltpu.VMEM((flat, width), jnp.bfloat16),
            pltpu.SemaphoreType.DMA((row_size,)),
            pltpu.SemaphoreType.DMA((row_size,)),
            pltpu.SemaphoreType.DMA((2,)),
            pltpu.SemaphoreType.DMA((2,)),
            pltpu.SemaphoreType.DMA((row_size,)),
            pltpu.SemaphoreType.DMA((row_size,)),
            pltpu.SemaphoreType.DMA,
            pltpu.SemaphoreType.DMA,
        ],
        compiler_params=pltpu.CompilerParams(
            collective_id=0, has_side_effects=True, vmem_limit_bytes=40 * 2**20
        ),
        cost_estimate=pl.CostEstimate(
            flops=10 * pairs * width, bytes_accessed=8 * flat * width, transcendentals=pairs
        ),
    )(
        queries,
        grad_out,
        attn_out,
        key_states,
        value_states,
        log_norm.T,
        position.reshape(-1, tokens),
        modality.reshape(-1, tokens),
        bidirectional,
    )


def solution(mesh):
    split = P(("row", "col"), None)
    return jax.shard_map(
        shards,
        mesh=mesh,
        in_specs=(split,) * 6 + (P(), P(), P()),
        out_specs=(split, split, split),
        check_vma=False,
    )
```

```python
import functools

import jax
import jax.numpy as jnp
from jax import lax
from jax.experimental import pallas as pl
from jax.experimental.pallas import tpu as pltpu
from jax.sharding import PartitionSpec as P

UNIT = 64
LOG2E = 1.4426950408889634
MASKED = -1e30
MESH = pl.DeviceIdType.MESH


def contract_first(left, right):
    return lax.dot_general(
        left, right, (((0,), (0,)), ((), ())), preferred_element_type=jnp.float32
    )


def contract_last(left, right):
    return lax.dot_general(
        left, right, (((1,), (1,)), ((), ())), preferred_element_type=jnp.float32
    )


def kernel(
    row_size,
    col_size,
    heads,
    q_hbm,
    d_hbm,
    o_hbm,
    k_hbm,
    v_hbm,
    lse_hbm,
    pos_hbm,
    mod_hbm,
    table_hbm,
    gq_ref,
    gk_ref,
    gv_ref,
    qd,
    aux,
    kv,
    acc,
    out_kv,
    in_kv,
    acc_q,
    out_q,
    in_q,
    kv_send,
    kv_recv,
    qd_send,
    qd_recv,
    grad_send,
    grad_recv,
    q_send,
    q_recv,
    o_ref,
    lse_ref,
    pos_ref,
    mod_ref,
    table_ref,
    load,
):
    me = lax.axis_index("row")
    col = lax.axis_index("col")
    mate = col + 1 - 2 * (col % 2)
    tokens, width = k_hbm.shape
    scale = width ** (-0.5)

    def ahead(step):
        return lax.rem(me + step, row_size)

    def behind(step):
        return lax.rem(me - step + row_size, row_size)

    sources = [(k_hbm, kv.at[0, 0]), (v_hbm, kv.at[0, 1])]
    for array, stacked in ((q_hbm, qd.at[0, 0]), (d_hbm, qd.at[0, 1]), (o_hbm, o_ref)):
        for h in range(heads):
            lanes = slice(h * width, (h + 1) * width)
            rows = slice(h * tokens, (h + 1) * tokens)
            sources.append((array.at[:, lanes], stacked.at[rows, :]))
    sources += [
        (lse_hbm, lse_ref),
        (pos_hbm, pos_ref),
        (mod_hbm, mod_ref),
        (table_hbm, table_ref),
    ]
    loads = [
        pltpu.make_async_copy(source, target, load.at[i])
        for i, (source, target) in enumerate(sources)
    ]
    for copy in loads:
        copy.start()
    kv_loads, qd_loads, other_loads = loads[:2], loads[2 : 2 + 2 * heads], loads[2 + 2 * heads :]

    barrier = pltpu.get_barrier_semaphore()

    def greet(step, carry):
        pl.semaphore_signal(barrier, inc=1, device_id={"row": ahead(step)}, device_id_type=MESH)
        return carry

    lax.fori_loop(1, row_size, greet, 0)
    pl.semaphore_signal(barrier, inc=1, device_id={"col": mate}, device_id_type=MESH)

    def kv_copy(step):
        return pltpu.make_async_remote_copy(
            src_ref=kv.at[0],
            dst_ref=kv.at[step],
            send_sem=kv_send.at[step],
            recv_sem=kv_recv.at[step],
            device_id={"row": ahead(step)},
            device_id_type=MESH,
        )

    def grad_copy(step):
        return pltpu.make_async_remote_copy(
            src_ref=out_kv.at[step],
            dst_ref=in_kv.at[step],
            send_sem=grad_send.at[step],
            recv_sem=grad_recv.at[step],
            device_id={"row": behind(step)},
            device_id_type=MESH,
        )

    def to_mate(source, target, send_sem, recv_sem):
        return pltpu.make_async_remote_copy(
            src_ref=source,
            dst_ref=target,
            send_sem=send_sem,
            recv_sem=recv_sem,
            device_id={"col": mate},
            device_id_type=MESH,
        )

    pair_copies = [
        to_mate(qd.at[0], qd.at[1], qd_send.at[0], qd_recv.at[0]),
        to_mate(aux.at[0], aux.at[1], qd_send.at[1], qd_recv.at[1]),
    ]
    q_copy = to_mate(out_q, in_q, q_send, q_recv)

    def send_kv(step, carry):
        kv_copy(step).start()
        return carry

    for copy in kv_loads:
        copy.wait()
    pl.semaphore_wait(barrier, row_size)
    lax.fori_loop(1, row_size, send_kv, 0)
    for copy in qd_loads:
        copy.wait()
    pair_copies[0].start()
    for copy in other_loads:
        copy.wait()
    for h in range(heads):
        rows = slice(h * tokens, (h + 1) * tokens)
        product = qd[0, 1, rows, :].astype(jnp.float32) * o_ref[rows, :].astype(jnp.float32)
        aux[0, heads + h : heads + h + 1, :] = jnp.sum(product.T, axis=0, keepdims=True)
    aux[0, 0:heads, :] = lse_ref[...] * LOG2E
    pair_copies[1].start()

    def limits(which_col):
        at = me * col_size + which_col
        pos = pos_ref[pl.ds(at, 1), :]
        mod = mod_ref[pl.ds(at, 1), :]
        last = pos - lax.rem(pos, UNIT) + (UNIT - 1)
        out = []
        for m in range(3):
            from_text, from_image, from_video = (table_ref[a : a + 1, m : m + 1] for a in range(3))
            seen = jnp.where(mod == 0, from_text, jnp.where(mod == 1, from_image, from_video))
            out.append(jnp.where(seen == 1, last, pos))
        return out

    def bias(step, limit):
        at = behind(step) * col_size + col
        shape = (tokens, tokens)
        pos = jnp.broadcast_to(pos_ref[pl.ds(at, 1), :], shape).T
        mod = jnp.broadcast_to(mod_ref[pl.ds(at, 1), :], shape).T
        bound = jnp.where(mod == 0, limit[0], jnp.where(mod == 1, limit[1], limit[2]))
        return jnp.where(pos <= bound, 0.0, MASKED)

    def tile(half, step, limit):
        flat_q = qd[half, 0]
        flat_d = qd[half, 1]
        keys = kv[step, 0]
        values = kv[step, 1]
        lse = jnp.concatenate([aux[half, h : h + 1, :] for h in range(heads)], axis=1)
        delta = jnp.concatenate(
            [aux[half, heads + h : heads + h + 1, :] for h in range(heads)], axis=1
        )
        hidden = jnp.concatenate([bias(step, limit)] * heads, axis=1)
        scores = contract_last(keys, flat_q)
        probs = jnp.exp2(scores * (scale * LOG2E) - lse + hidden)
        grad_probs = contract_last(values, flat_d)
        probs_low = probs.astype(jnp.bfloat16)
        scores_low = (probs * (grad_probs - delta)).astype(jnp.bfloat16)
        grad_v = jnp.dot(probs_low, flat_d, preferred_element_type=jnp.float32)
        grad_k = jnp.dot(scores_low, flat_q, preferred_element_type=jnp.float32)
        grad_q = contract_first(scores_low, keys)
        return grad_q, grad_k, grad_v

    acc_q[...] = jnp.zeros_like(acc_q)
    own_limit = limits(col)
    mate_limit = limits(mate)

    def own_step(step, carry):
        @pl.when(step > 0)
        def _():
            kv_copy(step).wait_recv()

        grad_q, grad_k, grad_v = tile(0, step, own_limit)
        acc_q[0] += grad_q
        acc[step, 0] = grad_k
        acc[step, 1] = grad_v
        return carry

    lax.fori_loop(0, row_size, own_step, 0)

    for copy in pair_copies:
        copy.wait_recv()

    def mate_step(i, carry):
        step = lax.rem(i + 1, row_size)
        grad_q, grad_k, grad_v = tile(1, step, mate_limit)
        acc_q[1] += grad_q
        grad_k = grad_k + acc[step, 0]
        grad_v = grad_v + acc[step, 1]

        @pl.when(step > 0)
        def _():
            out_kv[step, 0] = grad_k.astype(jnp.bfloat16)
            out_kv[step, 1] = grad_v.astype(jnp.bfloat16)
            grad_copy(step).start()

        @pl.when(step == 0)
        def _():
            acc[0, 0] = grad_k
            acc[0, 1] = grad_v

        return carry

    lax.fori_loop(0, row_size, mate_step, 0)

    out_q[...] = acc_q[1].astype(jnp.bfloat16)
    q_copy.start()

    def gather(step, carry):
        grad_copy(step).wait_recv()
        acc[0] += in_kv[step].astype(jnp.float32)
        return carry

    lax.fori_loop(1, row_size, gather, 0)
    gk_ref[...] = (acc[0, 0] * scale).astype(jnp.bfloat16)
    gv_ref[...] = acc[0, 1].astype(jnp.bfloat16)

    q_copy.wait_recv()
    for h in range(heads):
        rows = slice(h * tokens, (h + 1) * tokens)
        total = acc_q[0, rows, :] + in_q[rows, :].astype(jnp.float32)
        gq_ref[:, h * width : (h + 1) * width] = (total * scale).astype(jnp.bfloat16)

    def settle(step, carry):
        kv_copy(step).wait_send()
        grad_copy(step).wait_send()
        return carry

    lax.fori_loop(1, row_size, settle, 0)
    for copy in pair_copies:
        copy.wait_send()
    q_copy.wait_send()


def write_out(gq_ref, gk_ref, gv_ref, gq_hbm, gk_hbm, gv_hbm, sems):
    copies = [
        pltpu.make_async_copy(gq_ref, gq_hbm, sems.at[0]),
        pltpu.make_async_copy(gk_ref, gk_hbm, sems.at[1]),
        pltpu.make_async_copy(gv_ref, gv_hbm, sems.at[2]),
    ]
    for copy in copies:
        copy.start()
    for copy in copies:
        copy.wait()


def shards(
    queries,
    grad_out,
    attn_out,
    key_states,
    value_states,
    log_norm,
    position,
    modality,
    bidirectional,
):
    tokens, width = key_states.shape
    heads = log_norm.shape[1]
    row_size = lax.axis_size("row")
    col_size = lax.axis_size("col")
    flat = heads * tokens
    vmem = pl.BlockSpec(memory_space=pltpu.VMEM)
    hbm = pl.BlockSpec(memory_space=pltpu.HBM)
    pairs = row_size * tokens * flat * 2
    out_shape = (
        jax.ShapeDtypeStruct(queries.shape, jnp.bfloat16),
        jax.ShapeDtypeStruct(key_states.shape, jnp.bfloat16),
        jax.ShapeDtypeStruct(value_states.shape, jnp.bfloat16),
    )
    positions = position.reshape(-1, tokens)
    grads = pl.pallas_call(
        functools.partial(kernel, row_size, col_size, heads),
        out_shape=out_shape,
        in_specs=[hbm] * 9,
        out_specs=(vmem, vmem, vmem),
        scratch_shapes=[
            pltpu.VMEM((2, 2, flat, width), jnp.bfloat16),
            pltpu.VMEM((2, 2 * heads, tokens), jnp.float32),
            pltpu.VMEM((row_size, 2, tokens, width), jnp.bfloat16),
            pltpu.VMEM((row_size, 2, tokens, width), jnp.float32),
            pltpu.VMEM((row_size, 2, tokens, width), jnp.bfloat16),
            pltpu.VMEM((row_size, 2, tokens, width), jnp.bfloat16),
            pltpu.VMEM((2, flat, width), jnp.float32),
            pltpu.VMEM((flat, width), jnp.bfloat16),
            pltpu.VMEM((flat, width), jnp.bfloat16),
            pltpu.SemaphoreType.DMA((row_size,)),
            pltpu.SemaphoreType.DMA((row_size,)),
            pltpu.SemaphoreType.DMA((2,)),
            pltpu.SemaphoreType.DMA((2,)),
            pltpu.SemaphoreType.DMA((row_size,)),
            pltpu.SemaphoreType.DMA((row_size,)),
            pltpu.SemaphoreType.DMA,
            pltpu.SemaphoreType.DMA,
            pltpu.VMEM((flat, width), jnp.bfloat16),
            pltpu.VMEM((heads, tokens), jnp.float32),
            pltpu.VMEM(positions.shape, jnp.int32),
            pltpu.VMEM(positions.shape, jnp.int32),
            pltpu.VMEM(bidirectional.shape, jnp.int32),
            pltpu.SemaphoreType.DMA((3 * heads + 6,)),
        ],
        compiler_params=pltpu.CompilerParams(
            collective_id=0, has_side_effects=True, vmem_limit_bytes=40 * 2**20
        ),
        cost_estimate=pl.CostEstimate(
            flops=10 * pairs * width, bytes_accessed=8 * flat * width, transcendentals=pairs
        ),
    )(*(pltpu.with_memory_space_constraint(x, pltpu.HBM) for x in (
        queries,
        grad_out,
        attn_out,
        key_states,
        value_states,
        log_norm.T,
        positions,
        modality.reshape(-1, tokens),
        bidirectional,
    )))
    return pl.pallas_call(
        write_out,
        out_shape=out_shape,
        in_specs=[pl.BlockSpec(memory_space=pl.ANY)] * 3,
        out_specs=(hbm, hbm, hbm),
        scratch_shapes=[pltpu.SemaphoreType.DMA((3,))],
        compiler_params=pltpu.CompilerParams(vmem_limit_bytes=2**20),
    )(*grads)


def solution(mesh):
    split = P(("row", "col"), None)
    return jax.shard_map(
        shards,
        mesh=mesh,
        in_specs=(split,) * 6 + (P(), P(), P()),
        out_specs=(split, split, split),
        check_vma=False,
    )
```

```python
import functools

import jax
import jax.numpy as jnp
from jax import lax
from jax.experimental import pallas as pl
from jax.experimental.pallas import tpu as pltpu
from jax.sharding import PartitionSpec as P

UNIT = 64
LOG2E = 1.4426950408889634
MASKED = -1e30
MESH = pl.DeviceIdType.MESH


def contract_first(left, right):
    return lax.dot_general(
        left, right, (((0,), (0,)), ((), ())), preferred_element_type=jnp.float32
    )


def contract_last(left, right):
    return lax.dot_general(
        left, right, (((1,), (1,)), ((), ())), preferred_element_type=jnp.float32
    )


def kernel(
    row_size,
    col_size,
    heads,
    q_hbm,
    d_hbm,
    o_hbm,
    k_hbm,
    v_hbm,
    lse_hbm,
    pos_hbm,
    mod_hbm,
    table_hbm,
    gq_ref,
    gk_ref,
    gv_ref,
    qd,
    aux,
    kv,
    acc,
    out_sib,
    in_sib,
    out_kv,
    in_kv,
    acc_q,
    out_q,
    in_q,
    kv_send,
    kv_recv,
    sib_send,
    sib_recv,
    qd_send,
    qd_recv,
    grad_send,
    grad_recv,
    q_send,
    q_recv,
    o_ref,
    lse_ref,
    pos_ref,
    mod_ref,
    table_ref,
    load,
):
    me = lax.axis_index("row")
    col = lax.axis_index("col")
    mate = col + 1 - 2 * (col % 2)
    tokens, width = k_hbm.shape
    scale = width ** (-0.5)

    chips = row_size // 2
    chip, core = me // 2, lax.rem(me, 2)
    sibling = 2 * chip + 1 - core

    def ahead(c):
        return 2 * lax.rem(chip + c, chips) + core

    def behind(c, other=0):
        return 2 * lax.rem(chip - c + chips, chips) + (1 - core if other else core)

    sources = [(k_hbm, kv.at[0, 0]), (v_hbm, kv.at[0, 1])]
    for array, stacked in ((q_hbm, qd.at[0, 0]), (d_hbm, qd.at[0, 1]), (o_hbm, o_ref)):
        for h in range(heads):
            lanes = slice(h * width, (h + 1) * width)
            rows = slice(h * tokens, (h + 1) * tokens)
            sources.append((array.at[:, lanes], stacked.at[rows, :]))
    sources += [
        (lse_hbm, lse_ref),
        (pos_hbm, pos_ref),
        (mod_hbm, mod_ref),
        (table_hbm, table_ref),
    ]
    loads = [
        pltpu.make_async_copy(source, target, load.at[i])
        for i, (source, target) in enumerate(sources)
    ]
    for copy in loads:
        copy.start()
    kv_loads, qd_loads, other_loads = loads[:2], loads[2 : 2 + 2 * heads], loads[2 + 2 * heads :]

    barrier = pltpu.get_barrier_semaphore()

    def greet(step, carry):
        pl.semaphore_signal(barrier, inc=1, device_id={"row": ahead(step)}, device_id_type=MESH)
        return carry

    lax.fori_loop(1, chips, greet, 0)
    pl.semaphore_signal(barrier, inc=1, device_id={"row": sibling}, device_id_type=MESH)
    pl.semaphore_signal(barrier, inc=1, device_id={"col": mate}, device_id_type=MESH)

    def remote(source, target, send_sem, recv_sem, row):
        return pltpu.make_async_remote_copy(
            src_ref=source,
            dst_ref=target,
            send_sem=send_sem,
            recv_sem=recv_sem,
            device_id={"row": row},
            device_id_type=MESH,
        )

    def kv_copy(c):
        slot = 2 * c
        return remote(kv.at[0], kv.at[slot], kv_send.at[slot], kv_recv.at[slot], ahead(c))

    def kv_share(c):
        slot = 2 * c + 1
        return remote(kv.at[2 * c], kv.at[slot], kv_send.at[slot], kv_recv.at[slot], sibling)

    def grad_share(c):
        return remote(out_sib.at[c], in_sib.at[c], sib_send.at[c], sib_recv.at[c], sibling)

    def grad_copy(c):
        return remote(out_kv.at[c], in_kv.at[c], grad_send.at[c], grad_recv.at[c], behind(c))

    def to_mate(source, target, send_sem, recv_sem):
        return pltpu.make_async_remote_copy(
            src_ref=source,
            dst_ref=target,
            send_sem=send_sem,
            recv_sem=recv_sem,
            device_id={"col": mate},
            device_id_type=MESH,
        )

    pair_copies = [
        to_mate(qd.at[0], qd.at[1], qd_send.at[0], qd_recv.at[0]),
        to_mate(aux.at[0], aux.at[1], qd_send.at[1], qd_recv.at[1]),
    ]
    q_copy = to_mate(out_q, in_q, q_send, q_recv)

    def send_kv(step, carry):
        kv_copy(step).start()
        return carry

    for copy in kv_loads:
        copy.wait()
    pl.semaphore_wait(barrier, chips + 1)
    kv_share(0).start()
    lax.fori_loop(1, chips, send_kv, 0)
    for copy in qd_loads:
        copy.wait()
    pair_copies[0].start()
    for copy in other_loads:
        copy.wait()
    for h in range(heads):
        rows = slice(h * tokens, (h + 1) * tokens)
        product = qd[0, 1, rows, :].astype(jnp.float32) * o_ref[rows, :].astype(jnp.float32)
        aux[0, heads + h : heads + h + 1, :] = jnp.sum(product.T, axis=0, keepdims=True)
    aux[0, 0:heads, :] = lse_ref[...] * LOG2E
    pair_copies[1].start()

    def limits(which_col):
        at = me * col_size + which_col
        pos = pos_ref[pl.ds(at, 1), :]
        mod = mod_ref[pl.ds(at, 1), :]
        last = pos - lax.rem(pos, UNIT) + (UNIT - 1)
        out = []
        for m in range(3):
            from_text, from_image, from_video = (table_ref[a : a + 1, m : m + 1] for a in range(3))
            seen = jnp.where(mod == 0, from_text, jnp.where(mod == 1, from_image, from_video))
            out.append(jnp.where(seen == 1, last, pos))
        return out

    def bias(c, other, limit):
        at = behind(c, other) * col_size + col
        shape = (tokens, tokens)
        pos = jnp.broadcast_to(pos_ref[pl.ds(at, 1), :], shape).T
        mod = jnp.broadcast_to(mod_ref[pl.ds(at, 1), :], shape).T
        bound = jnp.where(mod == 0, limit[0], jnp.where(mod == 1, limit[1], limit[2]))
        return jnp.where(pos <= bound, 0.0, MASKED)

    def tile(half, c, limit):
        flat_q = qd[half, 0]
        flat_d = qd[half, 1]
        keys = kv[pl.ds(2 * c, 2), 0].reshape(2 * tokens, width)
        values = kv[pl.ds(2 * c, 2), 1].reshape(2 * tokens, width)
        lse = jnp.concatenate([aux[half, h : h + 1, :] for h in range(heads)], axis=1)
        delta = jnp.concatenate(
            [aux[half, heads + h : heads + h + 1, :] for h in range(heads)], axis=1
        )
        hidden = jnp.concatenate([bias(c, 0, limit), bias(c, 1, limit)], axis=0)
        hidden = jnp.concatenate([hidden] * heads, axis=1)
        scores = contract_last(keys, flat_q)
        probs = jnp.exp2(scores * (scale * LOG2E) - lse + hidden)
        grad_probs = contract_last(values, flat_d)
        probs_low = probs.astype(jnp.bfloat16)
        scores_low = (probs * (grad_probs - delta)).astype(jnp.bfloat16)
        grad_v = jnp.dot(probs_low, flat_d, preferred_element_type=jnp.float32)
        grad_k = jnp.dot(scores_low, flat_q, preferred_element_type=jnp.float32)
        grad_q = contract_first(scores_low, keys)
        return grad_q, grad_k, grad_v

    acc_q[...] = jnp.zeros_like(acc_q)
    own_limit = limits(col)
    mate_limit = limits(mate)

    def own_step(c, carry):
        kv_share(c).wait_recv()
        grad_q, grad_k, grad_v = tile(0, c, own_limit)
        acc_q[0] += grad_q
        for e in range(2):
            rows = slice(e * tokens, (e + 1) * tokens)
            acc[2 * c + e, 0] = grad_k[rows]
            acc[2 * c + e, 1] = grad_v[rows]
        return carry

    def share_kv(c, carry):
        kv_copy(c).wait_recv()
        kv_share(c).start()
        return carry

    lax.fori_loop(1, chips, share_kv, 0)
    lax.fori_loop(0, chips, own_step, 0)

    for copy in pair_copies:
        copy.wait_recv()

    def mate_step(i, carry):
        c = lax.rem(i + 1, chips)
        grad_q, grad_k, grad_v = tile(1, c, mate_limit)
        acc_q[1] += grad_q
        acc[2 * c, 0] += grad_k[:tokens]
        acc[2 * c, 1] += grad_v[:tokens]
        out_sib[c, 0] = (grad_k[tokens:] + acc[2 * c + 1, 0]).astype(jnp.bfloat16)
        out_sib[c, 1] = (grad_v[tokens:] + acc[2 * c + 1, 1]).astype(jnp.bfloat16)
        grad_share(c).start()

        @pl.when(i > 0)
        def _():
            grad_share(i).wait_recv()
            total = acc[2 * i] + in_sib[i].astype(jnp.float32)
            out_kv[i] = total.astype(jnp.bfloat16)
            grad_copy(i).start()

        return carry

    lax.fori_loop(0, chips, mate_step, 0)

    out_q[...] = acc_q[1].astype(jnp.bfloat16)
    q_copy.start()

    def gather(c, carry):
        grad_copy(c).wait_recv()
        acc[0] += in_kv[c].astype(jnp.float32)
        return carry

    grad_share(0).wait_recv()
    acc[0] += in_sib[0].astype(jnp.float32)
    lax.fori_loop(1, chips, gather, 0)
    gk_ref[...] = (acc[0, 0] * scale).astype(jnp.bfloat16)
    gv_ref[...] = acc[0, 1].astype(jnp.bfloat16)

    q_copy.wait_recv()
    for h in range(heads):
        rows = slice(h * tokens, (h + 1) * tokens)
        total = acc_q[0, rows, :] + in_q[rows, :].astype(jnp.float32)
        gq_ref[:, h * width : (h + 1) * width] = (total * scale).astype(jnp.bfloat16)

    def settle(step, carry):
        kv_copy(step).wait_send()
        kv_share(step).wait_send()
        grad_copy(step).wait_send()
        grad_share(step).wait_send()
        return carry

    kv_share(0).wait_send()
    grad_share(0).wait_send()
    lax.fori_loop(1, chips, settle, 0)
    for copy in pair_copies:
        copy.wait_send()
    q_copy.wait_send()


def write_out(gq_ref, gk_ref, gv_ref, gq_hbm, gk_hbm, gv_hbm, sems):
    copies = [
        pltpu.make_async_copy(gq_ref, gq_hbm, sems.at[0]),
        pltpu.make_async_copy(gk_ref, gk_hbm, sems.at[1]),
        pltpu.make_async_copy(gv_ref, gv_hbm, sems.at[2]),
    ]
    for copy in copies:
        copy.start()
    for copy in copies:
        copy.wait()


def shards(
    queries,
    grad_out,
    attn_out,
    key_states,
    value_states,
    log_norm,
    position,
    modality,
    bidirectional,
):
    tokens, width = key_states.shape
    heads = log_norm.shape[1]
    row_size = lax.axis_size("row")
    col_size = lax.axis_size("col")
    flat = heads * tokens
    chips = row_size // 2
    vmem = pl.BlockSpec(memory_space=pltpu.VMEM)
    hbm = pl.BlockSpec(memory_space=pltpu.HBM)
    pairs = row_size * tokens * flat * 2
    out_shape = (
        jax.ShapeDtypeStruct(queries.shape, jnp.bfloat16),
        jax.ShapeDtypeStruct(key_states.shape, jnp.bfloat16),
        jax.ShapeDtypeStruct(value_states.shape, jnp.bfloat16),
    )
    positions = position.reshape(-1, tokens)
    grads = pl.pallas_call(
        functools.partial(kernel, row_size, col_size, heads),
        out_shape=out_shape,
        in_specs=[hbm] * 9,
        out_specs=(vmem, vmem, vmem),
        scratch_shapes=[
            pltpu.VMEM((2, 2, flat, width), jnp.bfloat16),
            pltpu.VMEM((2, 2 * heads, tokens), jnp.float32),
            pltpu.VMEM((row_size, 2, tokens, width), jnp.bfloat16),
            pltpu.VMEM((row_size, 2, tokens, width), jnp.float32),
            pltpu.VMEM((chips, 2, tokens, width), jnp.bfloat16),
            pltpu.VMEM((chips, 2, tokens, width), jnp.bfloat16),
            pltpu.VMEM((chips, 2, tokens, width), jnp.bfloat16),
            pltpu.VMEM((chips, 2, tokens, width), jnp.bfloat16),
            pltpu.VMEM((2, flat, width), jnp.float32),
            pltpu.VMEM((flat, width), jnp.bfloat16),
            pltpu.VMEM((flat, width), jnp.bfloat16),
            pltpu.SemaphoreType.DMA((row_size,)),
            pltpu.SemaphoreType.DMA((row_size,)),
            pltpu.SemaphoreType.DMA((chips,)),
            pltpu.SemaphoreType.DMA((chips,)),
            pltpu.SemaphoreType.DMA((2,)),
            pltpu.SemaphoreType.DMA((2,)),
            pltpu.SemaphoreType.DMA((chips,)),
            pltpu.SemaphoreType.DMA((chips,)),
            pltpu.SemaphoreType.DMA,
            pltpu.SemaphoreType.DMA,
            pltpu.VMEM((flat, width), jnp.bfloat16),
            pltpu.VMEM((heads, tokens), jnp.float32),
            pltpu.VMEM(positions.shape, jnp.int32),
            pltpu.VMEM(positions.shape, jnp.int32),
            pltpu.VMEM(bidirectional.shape, jnp.int32),
            pltpu.SemaphoreType.DMA((3 * heads + 6,)),
        ],
        compiler_params=pltpu.CompilerParams(
            collective_id=0, has_side_effects=True, vmem_limit_bytes=40 * 2**20
        ),
        cost_estimate=pl.CostEstimate(
            flops=10 * pairs * width, bytes_accessed=8 * flat * width, transcendentals=pairs
        ),
    )(*(pltpu.with_memory_space_constraint(x, pltpu.HBM) for x in (
        queries,
        grad_out,
        attn_out,
        key_states,
        value_states,
        log_norm.T,
        positions,
        modality.reshape(-1, tokens),
        bidirectional,
    )))
    return pl.pallas_call(
        write_out,
        out_shape=out_shape,
        in_specs=[pl.BlockSpec(memory_space=pl.ANY)] * 3,
        out_specs=(hbm, hbm, hbm),
        scratch_shapes=[pltpu.SemaphoreType.DMA((3,))],
        compiler_params=pltpu.CompilerParams(vmem_limit_bytes=2**20),
    )(*grads)


def solution(mesh):
    split = P(("row", "col"), None)
    return jax.shard_map(
        shards,
        mesh=mesh,
        in_specs=(split,) * 6 + (P(), P(), P()),
        out_specs=(split, split, split),
        check_vma=False,
    )
```

```python
import functools

import jax
import jax.numpy as jnp
from jax import lax
from jax.experimental import pallas as pl
from jax.experimental.pallas import tpu as pltpu
from jax.sharding import PartitionSpec as P

UNIT = 64
LOG2E = 1.4426950408889634
MASKED = -1e30
MESH = pl.DeviceIdType.MESH


def contract_first(left, right):
    return lax.dot_general(
        left, right, (((0,), (0,)), ((), ())), preferred_element_type=jnp.float32
    )


def contract_last(left, right):
    return lax.dot_general(
        left, right, (((1,), (1,)), ((), ())), preferred_element_type=jnp.float32
    )


def kernel(
    row_size,
    col_size,
    heads,
    q_hbm,
    d_hbm,
    o_hbm,
    k_hbm,
    v_hbm,
    lse_hbm,
    pos_hbm,
    mod_hbm,
    table_hbm,
    gq_ref,
    gk_ref,
    gv_ref,
    qd,
    aux,
    kv,
    acc,
    out_sib,
    in_sib,
    out_kv,
    in_kv,
    acc_q,
    out_q,
    in_q,
    kv_send,
    kv_recv,
    sib_send,
    sib_recv,
    qd_send,
    qd_recv,
    grad_send,
    grad_recv,
    q_send,
    q_recv,
    o_ref,
    lse_ref,
    pos_ref,
    mod_ref,
    table_ref,
    load,
):
    me = lax.axis_index("row")
    col = lax.axis_index("col")
    mate = col + 1 - 2 * (col % 2)
    tokens, width = k_hbm.shape
    scale = width ** (-0.5)

    chips = row_size // 2
    chip, core = me // 2, lax.rem(me, 2)
    sibling = 2 * chip + 1 - core

    def ahead(c):
        return 2 * lax.rem(chip + c, chips) + core

    def behind(c, other=0):
        return 2 * lax.rem(chip - c + chips, chips) + (1 - core if other else core)

    sources = [(k_hbm, kv.at[0, 0]), (v_hbm, kv.at[0, 1])]
    for array, stacked in ((q_hbm, qd.at[0, 0]), (d_hbm, qd.at[0, 1]), (o_hbm, o_ref)):
        for h in range(heads):
            lanes = slice(h * width, (h + 1) * width)
            rows = slice(h * tokens, (h + 1) * tokens)
            sources.append((array.at[:, lanes], stacked.at[rows, :]))
    sources += [
        (lse_hbm, lse_ref),
        (pos_hbm, pos_ref),
        (mod_hbm, mod_ref),
        (table_hbm, table_ref),
    ]
    loads = [
        pltpu.make_async_copy(source, target, load.at[i])
        for i, (source, target) in enumerate(sources)
    ]
    for copy in loads:
        copy.start()
    kv_loads, qd_loads, other_loads = loads[:2], loads[2 : 2 + 2 * heads], loads[2 + 2 * heads :]

    barrier = pltpu.get_barrier_semaphore()

    def greet(step, carry):
        pl.semaphore_signal(barrier, inc=1, device_id={"row": ahead(step)}, device_id_type=MESH)
        return carry

    lax.fori_loop(1, chips, greet, 0)
    pl.semaphore_signal(barrier, inc=1, device_id={"row": sibling}, device_id_type=MESH)
    pl.semaphore_signal(barrier, inc=1, device_id={"col": mate}, device_id_type=MESH)

    def remote(source, target, send_sem, recv_sem, row):
        return pltpu.make_async_remote_copy(
            src_ref=source,
            dst_ref=target,
            send_sem=send_sem,
            recv_sem=recv_sem,
            device_id={"row": row},
            device_id_type=MESH,
        )

    def kv_copy(c):
        slot = 2 * c
        return remote(kv.at[0], kv.at[slot], kv_send.at[slot], kv_recv.at[slot], ahead(c))

    def kv_share(c):
        slot = 2 * c + 1
        return remote(kv.at[2 * c], kv.at[slot], kv_send.at[slot], kv_recv.at[slot], sibling)

    def grad_share(c):
        return remote(out_sib.at[c], in_sib.at[c], sib_send.at[c], sib_recv.at[c], sibling)

    def grad_copy(c):
        return remote(out_kv.at[c], in_kv.at[c], grad_send.at[c], grad_recv.at[c], behind(c))

    def to_mate(source, target, send_sem, recv_sem):
        return pltpu.make_async_remote_copy(
            src_ref=source,
            dst_ref=target,
            send_sem=send_sem,
            recv_sem=recv_sem,
            device_id={"col": mate},
            device_id_type=MESH,
        )

    pair_copies = [
        to_mate(qd.at[0], qd.at[1], qd_send.at[0], qd_recv.at[0]),
        to_mate(aux.at[0], aux.at[1], qd_send.at[1], qd_recv.at[1]),
    ]
    q_copy = to_mate(out_q, in_q, q_send, q_recv)

    def send_kv(step, carry):
        kv_copy(step).start()
        return carry

    for copy in kv_loads:
        copy.wait()
    pl.semaphore_wait(barrier, chips + 1)
    kv_share(0).start()
    lax.fori_loop(1, chips, send_kv, 0)
    for copy in qd_loads:
        copy.wait()
    pair_copies[0].start()
    for copy in other_loads:
        copy.wait()
    for h in range(heads):
        rows = slice(h * tokens, (h + 1) * tokens)
        product = qd[0, 1, rows, :].astype(jnp.float32) * o_ref[rows, :].astype(jnp.float32)
        aux[0, heads + h : heads + h + 1, :] = jnp.sum(product.T, axis=0, keepdims=True)
    aux[0, 0:heads, :] = lse_ref[...] * LOG2E
    pair_copies[1].start()

    def limits(which_col):
        at = me * col_size + which_col
        pos = pos_ref[pl.ds(at, 1), :]
        mod = mod_ref[pl.ds(at, 1), :]
        last = pos - lax.rem(pos, UNIT) + (UNIT - 1)
        out = []
        for m in range(3):
            from_text, from_image, from_video = (table_ref[a : a + 1, m : m + 1] for a in range(3))
            seen = jnp.where(mod == 0, from_text, jnp.where(mod == 1, from_image, from_video))
            out.append(jnp.where(seen == 1, last, pos))
        return out

    def bias(c, other, limit):
        at = behind(c, other) * col_size + col
        shape = (tokens, tokens)
        pos = jnp.broadcast_to(pos_ref[pl.ds(at, 1), :], shape).T
        mod = jnp.broadcast_to(mod_ref[pl.ds(at, 1), :], shape).T
        bound = jnp.where(mod == 0, limit[0], jnp.where(mod == 1, limit[1], limit[2]))
        return jnp.where(pos <= bound, 0.0, MASKED)

    def tile(half, c, limit):
        flat_q = qd[half, 0]
        flat_d = qd[half, 1]
        keys = kv[pl.ds(2 * c, 2), 0].reshape(2 * tokens, width)
        values = kv[pl.ds(2 * c, 2), 1].reshape(2 * tokens, width)
        lse = jnp.concatenate([aux[half, h : h + 1, :] for h in range(heads)], axis=1)
        delta = jnp.concatenate(
            [aux[half, heads + h : heads + h + 1, :] for h in range(heads)], axis=1
        )
        hidden = jnp.concatenate([bias(c, 0, limit), bias(c, 1, limit)], axis=0)
        hidden = jnp.concatenate([hidden] * heads, axis=1)
        scores = contract_last(keys, flat_q)
        probs = jnp.exp2(scores * (scale * LOG2E) - lse + hidden)
        grad_probs = contract_last(values, flat_d)
        probs_low = probs.astype(jnp.bfloat16)
        scores_low = (probs * (grad_probs - delta)).astype(jnp.bfloat16)
        grad_v = jnp.dot(probs_low, flat_d, preferred_element_type=jnp.float32)
        grad_k = jnp.dot(scores_low, flat_q, preferred_element_type=jnp.float32)
        grad_q = contract_first(scores_low, keys)
        return grad_q, grad_k, grad_v

    acc_q[...] = jnp.zeros_like(acc_q)
    own_limit = limits(col)
    mate_limit = limits(mate)

    def own_step(c, carry):
        kv_share(c).wait_recv()
        grad_q, grad_k, grad_v = tile(0, c, own_limit)
        acc_q[0] += grad_q
        for e in range(2):
            rows = slice(e * tokens, (e + 1) * tokens)
            acc[2 * c + e, 0] = grad_k[rows]
            acc[2 * c + e, 1] = grad_v[rows]
        return carry

    def share_kv(c, carry):
        kv_copy(c).wait_recv()
        kv_share(c).start()
        return carry

    own_step(0, 0)
    lax.fori_loop(1, chips, share_kv, 0)
    lax.fori_loop(1, chips, own_step, 0)

    for copy in pair_copies:
        copy.wait_recv()

    def pass_on(c):
        grad_share(c).wait_recv()
        total = acc[2 * c] + in_sib[c].astype(jnp.float32)
        out_kv[c] = total.astype(jnp.bfloat16)
        grad_copy(c).start()

    def mate_step(i, carry):
        c = lax.rem(i + 1, chips)
        grad_q, grad_k, grad_v = tile(1, c, mate_limit)
        acc_q[1] += grad_q
        acc[2 * c, 0] += grad_k[:tokens]
        acc[2 * c, 1] += grad_v[:tokens]
        out_sib[c, 0] = (grad_k[tokens:] + acc[2 * c + 1, 0]).astype(jnp.bfloat16)
        out_sib[c, 1] = (grad_v[tokens:] + acc[2 * c + 1, 1]).astype(jnp.bfloat16)
        grad_share(c).start()

        @pl.when(i > 1)
        def _():
            pass_on(i - 1)

        return carry

    lax.fori_loop(0, chips, mate_step, 0)

    out_q[...] = acc_q[1].astype(jnp.bfloat16)
    q_copy.start()
    if chips > 1:
        pass_on(chips - 1)

    def gather(c, carry):
        grad_copy(c).wait_recv()
        acc[0] += in_kv[c].astype(jnp.float32)
        return carry

    grad_share(0).wait_recv()
    acc[0] += in_sib[0].astype(jnp.float32)
    lax.fori_loop(1, chips, gather, 0)
    gk_ref[...] = (acc[0, 0] * scale).astype(jnp.bfloat16)
    gv_ref[...] = acc[0, 1].astype(jnp.bfloat16)

    q_copy.wait_recv()
    for h in range(heads):
        rows = slice(h * tokens, (h + 1) * tokens)
        total = acc_q[0, rows, :] + in_q[rows, :].astype(jnp.float32)
        gq_ref[:, h * width : (h + 1) * width] = (total * scale).astype(jnp.bfloat16)

    def settle(step, carry):
        kv_copy(step).wait_send()
        kv_share(step).wait_send()
        grad_copy(step).wait_send()
        grad_share(step).wait_send()
        return carry

    kv_share(0).wait_send()
    grad_share(0).wait_send()
    lax.fori_loop(1, chips, settle, 0)
    for copy in pair_copies:
        copy.wait_send()
    q_copy.wait_send()


def write_out(gq_ref, gk_ref, gv_ref, gq_hbm, gk_hbm, gv_hbm, sems):
    copies = [
        pltpu.make_async_copy(gq_ref, gq_hbm, sems.at[0]),
        pltpu.make_async_copy(gk_ref, gk_hbm, sems.at[1]),
        pltpu.make_async_copy(gv_ref, gv_hbm, sems.at[2]),
    ]
    for copy in copies:
        copy.start()
    for copy in copies:
        copy.wait()


def shards(
    queries,
    grad_out,
    attn_out,
    key_states,
    value_states,
    log_norm,
    position,
    modality,
    bidirectional,
):
    tokens, width = key_states.shape
    heads = log_norm.shape[1]
    row_size = lax.axis_size("row")
    col_size = lax.axis_size("col")
    flat = heads * tokens
    chips = row_size // 2
    vmem = pl.BlockSpec(memory_space=pltpu.VMEM)
    hbm = pl.BlockSpec(memory_space=pltpu.HBM)
    pairs = row_size * tokens * flat * 2
    out_shape = (
        jax.ShapeDtypeStruct(queries.shape, jnp.bfloat16),
        jax.ShapeDtypeStruct(key_states.shape, jnp.bfloat16),
        jax.ShapeDtypeStruct(value_states.shape, jnp.bfloat16),
    )
    positions = position.reshape(-1, tokens)
    grads = pl.pallas_call(
        functools.partial(kernel, row_size, col_size, heads),
        out_shape=out_shape,
        in_specs=[hbm] * 9,
        out_specs=(vmem, vmem, vmem),
        scratch_shapes=[
            pltpu.VMEM((2, 2, flat, width), jnp.bfloat16),
            pltpu.VMEM((2, 2 * heads, tokens), jnp.float32),
            pltpu.VMEM((row_size, 2, tokens, width), jnp.bfloat16),
            pltpu.VMEM((row_size, 2, tokens, width), jnp.float32),
            pltpu.VMEM((chips, 2, tokens, width), jnp.bfloat16),
            pltpu.VMEM((chips, 2, tokens, width), jnp.bfloat16),
            pltpu.VMEM((chips, 2, tokens, width), jnp.bfloat16),
            pltpu.VMEM((chips, 2, tokens, width), jnp.bfloat16),
            pltpu.VMEM((2, flat, width), jnp.float32),
            pltpu.VMEM((flat, width), jnp.bfloat16),
            pltpu.VMEM((flat, width), jnp.bfloat16),
            pltpu.SemaphoreType.DMA((row_size,)),
            pltpu.SemaphoreType.DMA((row_size,)),
            pltpu.SemaphoreType.DMA((chips,)),
            pltpu.SemaphoreType.DMA((chips,)),
            pltpu.SemaphoreType.DMA((2,)),
            pltpu.SemaphoreType.DMA((2,)),
            pltpu.SemaphoreType.DMA((chips,)),
            pltpu.SemaphoreType.DMA((chips,)),
            pltpu.SemaphoreType.DMA,
            pltpu.SemaphoreType.DMA,
            pltpu.VMEM((flat, width), jnp.bfloat16),
            pltpu.VMEM((heads, tokens), jnp.float32),
            pltpu.VMEM(positions.shape, jnp.int32),
            pltpu.VMEM(positions.shape, jnp.int32),
            pltpu.VMEM(bidirectional.shape, jnp.int32),
            pltpu.SemaphoreType.DMA((3 * heads + 6,)),
        ],
        compiler_params=pltpu.CompilerParams(
            collective_id=0, has_side_effects=True, vmem_limit_bytes=40 * 2**20
        ),
        cost_estimate=pl.CostEstimate(
            flops=10 * pairs * width, bytes_accessed=8 * flat * width, transcendentals=pairs
        ),
    )(*(pltpu.with_memory_space_constraint(x, pltpu.HBM) for x in (
        queries,
        grad_out,
        attn_out,
        key_states,
        value_states,
        log_norm.T,
        positions,
        modality.reshape(-1, tokens),
        bidirectional,
    )))
    return pl.pallas_call(
        write_out,
        out_shape=out_shape,
        in_specs=[pl.BlockSpec(memory_space=pl.ANY)] * 3,
        out_specs=(hbm, hbm, hbm),
        scratch_shapes=[pltpu.SemaphoreType.DMA((3,))],
        compiler_params=pltpu.CompilerParams(vmem_limit_bytes=2**20),
    )(*grads)


def solution(mesh):
    split = P(("row", "col"), None)
    return jax.shard_map(
        shards,
        mesh=mesh,
        in_specs=(split,) * 6 + (P(), P(), P()),
        out_specs=(split, split, split),
        check_vma=False,
    )
```
